32 devices in a mesh: sec: 8 (over y, x, core), day: 4 (over z).
Axes of the slice: x: 2, y: 2, z: 4, core: 2. Of those that a mesh axis runs over, the one named last changes fastest.
Arguments:
- sec_pnl: bfloat16 [8192, 2048], P('sec', 'day'), may hold values from -6 to 6
- holdings: bfloat16 [128, 128, 128], P('sec'), may hold values from -0.109375 to 0.109375
- tile_pblock: int32 [128], P('sec'), may hold values from 0 to 1, as said below
- tile_sblock: int32 [128], P('sec'), may hold values from 0 to 7
- tile_count: int32 [8], P('sec'), may hold values from 4 to 16, as said below
- tail_days: int32 [256, 103], replicated, may hold values from 0 to 2047, as said below
Outputs:
- pnl: bfloat16 [256, 2048], P('sec', 'day')
- shortfall: float32 [256], P('sec')
- tail_mean: float32 [128, 128, 128], P(('sec', 'day'))
The draws below stay inside these ranges and needn't reach their ends.
Inputs may be any that keep to these rules, and one draw needn't show every extreme that they name: On each security device the pairs (tile_pblock, tile_sblock) of its 16 slots are distinct. `tile_count`: some security device has all 16 slots live in every draw. `tail_days`: each row holds 103 distinct days.
All inputs are finite; a program needn't handle non-finite values.
Results may differ from the reference program's by a relative error of at most 0.0015.
Values may be sent and summed in bfloat16 or wider, within the bound.
A program may use at most 64 MiB of HBM per device.

```python
import jax
import jax.numpy as jnp
from jax import lax

SB = 128
PB = 128
DAYS = 2048
TAIL = 103
SBLK_DEV = 8
PBLK = 2
CAP = 16
TILES = 128
SECS = 8192
N_SEC = 8


def tile_pairs(key):
    keys = jax.random.split(jax.random.fold_in(key, 7), N_SEC)

    def one_device(sub):
        order = jax.random.permutation(sub, PBLK * SBLK_DEV)[:CAP]
        return order.astype(jnp.int32)
    pairs = jax.vmap(one_device)(keys).reshape(-1)
    return (pairs // SBLK_DEV, pairs % SBLK_DEV)


def draw_tile_pblock(key, part):
    return tile_pairs(key)[0].astype(jnp.int32)


def draw_tile_sblock(key, part):
    return tile_pairs(key)[1].astype(jnp.int32)


def draw_tile_count(key, part):
    first, second = jax.random.split(jax.random.fold_in(key, 11))
    counts = jax.random.randint(first, (N_SEC,), CAP // 4, CAP // 2 + 1, dtype=jnp.int32)
    busiest = jax.random.randint(second, (), 0, N_SEC, dtype=jnp.int32)
    places = jnp.arange(N_SEC, dtype=jnp.int32)
    return jnp.where(places == busiest, CAP, counts).astype(jnp.int32)


def draw_tail_days(key, part):
    keys = jax.random.split(jax.random.fold_in(key, 13), PBLK * PB)

    def one_row(sub):
        return jax.random.permutation(sub, DAYS)[:TAIL].astype(jnp.int32)
    return jax.vmap(one_row)(keys)


def levels(own_key, dims, shards, low, largest):
    def one(axis_at, blocks):
        draws = jax.random.uniform(jax.random.fold_in(jax.random.fold_in(own_key, 6), axis_at), (blocks,), jnp.float32, low / len(shards), largest / len(shards))
        return jnp.repeat(jnp.exp(draws), dims[axis_at] // blocks).reshape((-1,) + (1,) * (len(dims) - axis_at - 1))

    factor_of = one(*shards[0])
    for cut in shards[1:]:
        factor_of = factor_of * one(*cut)
    return factor_of


def centred(stream_key, extent, spread, bound, cuts=(), held_as=jnp.bfloat16):
    level = levels(stream_key, extent, cuts, -0.22, 0.18) if cuts else 1.0
    array = jax.random.normal(stream_key, extent, jnp.float32) * spread * level
    return jnp.minimum(jnp.maximum(array, -bound), bound).astype(held_as)


def setup_inputs(seed: int = 0) -> dict:
    streams_of = jax.random.split(jax.random.key(seed), 7)
    sec_pnl = centred(streams_of[0], (SECS, DAYS), 1.0, 6.0, ((0, 8), (1, 4)))
    holdings = centred(streams_of[1], (TILES, PB, SB), (CAP * N_SEC * SB // PBLK // 3) ** -0.5, 0.109375, ((0, 8),))
    tile_pblock = draw_tile_pblock(jax.random.fold_in(streams_of[6], 71), 0)
    tile_sblock = draw_tile_sblock(jax.random.fold_in(streams_of[6], 71), 0)
    tile_count = draw_tile_count(jax.random.fold_in(streams_of[6], 71), 0)
    tail_days = draw_tail_days(jax.random.fold_in(streams_of[6], 71), 0)
    return {"sec_pnl": sec_pnl, "holdings": holdings, "tile_pblock": tile_pblock, "tile_sblock": tile_sblock, "tile_count": tile_count, "tail_days": tail_days}


def reference(sec_pnl, holdings, tile_pblock, tile_sblock, tile_count, tail_days):
    slots_all = holdings.shape[0]
    positions = jnp.arange(slots_all, dtype=jnp.int32)
    device_of = positions // CAP
    alive = ((positions % CAP) < tile_count[device_of]).astype(jnp.float32)
    global_block = (device_of * SBLK_DEV + tile_sblock).astype(jnp.int32)

    def step(total, item):
        tile, pblock, sblock, flag = item
        block = lax.dynamic_slice_in_dim(sec_pnl, (sblock * SB).astype(jnp.int32), SB, 0)
        piece = jnp.dot(tile, block, preferred_element_type=jnp.float32) * flag
        start = (pblock * PB).astype(jnp.int32)
        current = lax.dynamic_slice_in_dim(total, start, PB, 0)
        return lax.dynamic_update_slice_in_dim(total, current + piece, start, 0), None

    total, _ = lax.scan(step, jnp.zeros((PBLK * PB, DAYS), jnp.float32),
                        (holdings, tile_pblock, global_block, alive))
    pnl = total.astype(jnp.bfloat16)
    picked = jnp.take_along_axis(total, tail_days.astype(jnp.int32), axis=1)
    shortfall = -jnp.sum(picked, axis=1) / TAIL

    def one_tile(item):
        pblock, sblock, flag = item
        block = lax.dynamic_slice_in_dim(sec_pnl, (sblock * SB).astype(jnp.int32), SB, 0).astype(jnp.float32)
        chosen = lax.dynamic_slice_in_dim(tail_days, (pblock * PB).astype(jnp.int32), PB, 0)
        values = jnp.take(block, chosen.astype(jnp.int32), axis=1)
        return jnp.sum(values, axis=2).T * flag / TAIL

    tail_mean = lax.map(one_tile, (tile_pblock, global_block, alive))
    return pnl, shortfall, tail_mean
```

```python
import functools

import jax
import jax.numpy as jnp
from jax import lax
from jax.experimental import pallas as pl
from jax.experimental.pallas import tpu as pltpu
from jax.sharding import PartitionSpec as P

SB = 128
PB = 128
WORDS = 16
WIRE = jnp.int16
REACH = 32767.0
F32 = jnp.float32
MESH = pl.DeviceIdType.MESH


def kernel(
    n_sec,
    n_day,
    pblock_ref,
    sblock_ref,
    count_ref,
    sec_ref,
    hold_ref,
    days_ref,
    pnl_ref,
    short_ref,
    tail_ref,
    dense,
    held,
    part,
    share_in,
    mask_t,
    tail_own,
    tail_out,
    tail_in,
    peak_out,
    peak_in,
    pick_out,
    pick_in,
    share_send,
    share_recv,
    tail_send,
    tail_recv,
    peak_send,
    peak_recv,
    pick_send,
    pick_recv,
):
    sec, day = lax.axis_index("sec"), lax.axis_index("day")
    sblocks, _, width = sec_ref.shape
    slots = hold_ref.shape[0]
    portfolios, tail = days_ref.shape
    pblocks = portfolios // PB
    rows = portfolios // n_sec
    own = slots // n_day
    bits = width // WORDS

    barrier = pltpu.get_barrier_semaphore()
    for r in range(1, n_sec):
        pl.semaphore_signal(
            barrier, inc=1, device_id={"sec": lax.rem(sec + r, n_sec)}, device_id_type=MESH
        )
    for r in range(1, n_day):
        pl.semaphore_signal(
            barrier, inc=1, device_id={"day": lax.rem(day + r, n_day)}, device_id_type=MESH
        )

    here = jnp.transpose(days_ref[...]) - day * width
    inside = (here >= 0) & (here < width)
    word = jnp.where(inside, here & (WORDS - 1), -1)
    bit = jnp.left_shift(1, jnp.where(inside, here >> 4, 0))
    which = lax.broadcasted_iota(jnp.int32, (WORDS, portfolios), 0)
    packed = jnp.zeros((WORDS, portfolios), jnp.int32)
    for k in range(tail):
        packed = packed | jnp.where(which == word[k : k + 1, :], bit[k : k + 1, :], 0)
    for b in range(bits):
        piece = ((packed >> b) & 1).astype(F32).astype(jnp.bfloat16)
        for p in range(pblocks):
            mask_t[p, b * WORDS : (b + 1) * WORDS, :] = piece[:, p * PB : (p + 1) * PB]

    peak_out[...] = jnp.zeros(peak_out.shape, F32)

    pl.semaphore_wait(barrier, n_sec - 1 + n_day - 1)

    def tail_sum(slot):
        block = sec_ref[sblock_ref[slot]]
        return jnp.dot(block, mask_t[pblock_ref[slot]], preferred_element_type=F32)

    sends = []

    def send(src, dst, send_sem, recv_sem, where):
        copy = pltpu.make_async_remote_copy(
            src_ref=src,
            dst_ref=dst,
            send_sem=send_sem,
            recv_sem=recv_sem,
            device_id=where,
            device_id_type=MESH,
        )
        copy.start()
        sends.append(copy)
        return copy

    peak_copies, tail_copies = {}, {}
    for i in range(own):
        for r in range(1, n_day):
            to = lax.rem(day + r, n_day)
            at = (r - 1) * own + i
            sums = tail_sum(to * own + i)
            peak = jnp.maximum(jnp.max(jnp.abs(sums), axis=0, keepdims=True), 1e-30)
            peak_out[r - 1, i : i + 1, :] = peak
            tail_out[at] = jnp.round(sums * (REACH / peak)).astype(jnp.int32).astype(WIRE)
            tail_copies[r, i] = send(
                tail_out.at[at], tail_in.at[at], tail_send.at[at], tail_recv.at[at], {"day": to}
            )
    for r in range(1, n_day):
        to = lax.rem(day + r, n_day)
        peak_copies[r] = send(
            peak_out.at[r - 1], peak_in.at[r - 1], peak_send.at[r - 1], peak_recv.at[r - 1],
            {"day": to},
        )

    for t in range(slots):
        tile = hold_ref[t]
        home = jnp.where(t < count_ref[0], pblock_ref[t], -1)
        for p in range(pblocks):
            keep = (jnp.full((1, SB), home, jnp.int32) == p).astype(F32).astype(jnp.bfloat16)
            dense[p * PB : (p + 1) * PB, t * SB : (t + 1) * SB] = tile * keep
        held[t * SB : (t + 1) * SB, :] = sec_ref[sblock_ref[t]]
    part[...] = jnp.dot(dense[...], held[...], preferred_element_type=F32)

    share_copies = []
    for r in range(1, n_sec):
        to = lax.rem(sec + r, n_sec)
        share_copies.append(
            send(
                part.at[pl.ds(pl.multiple_of(to * rows, rows), rows), :],
                share_in.at[r - 1],
                share_send.at[r - 1],
                share_recv.at[r - 1],
                {"sec": to},
            )
        )

    for i in range(own):
        tail_own[i] = tail_sum(day * own + i)

    share = part[pl.ds(pl.multiple_of(sec * rows, rows), rows), :]
    for r in range(1, n_sec):
        share_copies[r - 1].wait_recv()
        share = share + share_in[r - 1]
    pnl_ref[...] = share.astype(jnp.bfloat16)
    high = share.astype(jnp.bfloat16)
    low = (share - high.astype(F32)).astype(jnp.bfloat16)
    lane = lax.broadcasted_iota(jnp.int32, (rows, PB), 1)
    line = lax.broadcasted_iota(jnp.int32, (rows, PB), 0)
    picked = []
    for p in range(pblocks):
        sums = jnp.dot(high, mask_t[p], preferred_element_type=F32)
        sums = sums + jnp.dot(low, mask_t[p], preferred_element_type=F32)
        mine = lane + p * PB == line + sec * rows
        picked.append(jnp.sum(jnp.where(mine, sums, 0.0), axis=0, keepdims=True))
    pick_out[...] = jnp.broadcast_to(jnp.concatenate(picked, axis=1), pick_out.shape)
    pick_copies = {}
    for r in range(1, n_day):
        to = lax.rem(day + r, n_day)
        pick_copies[r] = send(
            pick_out, pick_in.at[r - 1], pick_send.at[r - 1], pick_recv.at[r - 1], {"day": to}
        )

    back = {}
    for r in range(1, n_day):
        peak_copies[r].wait_recv()
        back[r] = peak_in[r - 1] * (1.0 / REACH)
    for i in range(own):
        total = tail_own[i]
        for r in range(1, n_day):
            tail_copies[r, i].wait_recv()
            coded = tail_in[(r - 1) * own + i].astype(jnp.int32).astype(F32)
            total = total + coded * back[r][i : i + 1, :]
        live = jnp.where(day * own + i < count_ref[0], 1.0, 0.0)
        tail_ref[i] = jnp.transpose(total) * (live / tail)

    lost = pick_out[...]
    for r in range(1, n_day):
        pick_copies[r].wait_recv()
        lost = lost + pick_in[r - 1]
    turned = pltpu.roll(lost, lax.rem(portfolios - sec * rows, portfolios), 1)
    short_ref[...] = turned[0:1, 0:rows] * (-1.0 / tail)
    for copy in sends:
        copy.wait_send()


def local(n_sec, n_day, sec_pnl, holdings, tile_pblock, tile_sblock, tile_count, tail_days):
    width = sec_pnl.shape[1]
    slots = holdings.shape[0]
    portfolios = tail_days.shape[0]
    rows, own = portfolios // n_sec, slots // n_day
    far = n_day - 1
    peak_rows = -(-own // 8) * 8
    smem, vmem = pl.BlockSpec(memory_space=pltpu.SMEM), pl.BlockSpec(memory_space=pltpu.VMEM)
    dma = pltpu.SemaphoreType.DMA
    pnl, short, tail = pl.pallas_call(
        functools.partial(kernel, n_sec, n_day),
        out_shape=(
            jax.ShapeDtypeStruct((rows, width), jnp.bfloat16),
            jax.ShapeDtypeStruct((1, rows), F32),
            jax.ShapeDtypeStruct((own, PB, SB), F32),
        ),
        in_specs=[smem] * 3 + [vmem] * 3,
        out_specs=(vmem, vmem, vmem),
        scratch_shapes=[
            pltpu.VMEM((portfolios, slots * SB), jnp.bfloat16),
            pltpu.VMEM((slots * SB, width), jnp.bfloat16),
            pltpu.VMEM((portfolios, width), F32),
            pltpu.VMEM((n_sec - 1, rows, width), F32),
            pltpu.VMEM((portfolios // PB, width, PB), jnp.bfloat16),
            pltpu.VMEM((own, SB, PB), F32),
            pltpu.VMEM((far * own, SB, PB), WIRE),
            pltpu.VMEM((far * own, SB, PB), WIRE),
            pltpu.VMEM((far, peak_rows, PB), F32),
            pltpu.VMEM((far, peak_rows, PB), F32),
            pltpu.VMEM((8, portfolios), F32),
            pltpu.VMEM((far, 8, portfolios), F32),
            dma((n_sec - 1,)),
            dma((n_sec - 1,)),
            dma((far * own,)),
            dma((far * own,)),
            dma((far,)),
            dma((far,)),
            dma((far,)),
            dma((far,)),
        ],
        compiler_params=pltpu.CompilerParams(
            collective_id=0, has_side_effects=True, vmem_limit_bytes=40 * 1024 * 1024
        ),
    )(tile_pblock, tile_sblock, tile_count, sec_pnl.reshape(-1, SB, width), holdings, tail_days)
    return pnl, short.reshape(rows), tail


def solution(mesh):
    placed = (P("sec", "day"), P("sec", None, None), P("sec"), P("sec"), P("sec"), P())
    return jax.shard_map(
        functools.partial(local, mesh.shape["sec"], mesh.shape["day"]),
        mesh=mesh,
        in_specs=placed,
        out_specs=(P("sec", "day"), P("sec"), P(("sec", "day"), None, None)),
        check_vma=False,
    )
```

```python
import functools

import jax
import jax.numpy as jnp
from jax import lax
from jax.experimental import pallas as pl
from jax.experimental.pallas import tpu as pltpu
from jax.sharding import PartitionSpec as P

SB = 128
PB = 128
WORDS = 16
WIRE = jnp.int16
REACH = 32767.0
F32 = jnp.float32
MESH = pl.DeviceIdType.MESH


def kernel(
    n_sec,
    n_day,
    pblock_ref,
    sblock_ref,
    count_ref,
    sec_hbm,
    hold_hbm,
    days_hbm,
    pnl_ref,
    short_ref,
    tail_ref,
    sec_ref,
    hold_ref,
    days_ref,
    dense,
    held,
    part,
    share_in,
    mask_t,
    tail_own,
    tail_out,
    tail_in,
    peak_out,
    peak_in,
    pick_out,
    pick_in,
    load,
    share_send,
    share_recv,
    tail_send,
    tail_recv,
    peak_send,
    peak_recv,
    pick_send,
    pick_recv,
):
    sec, day = lax.axis_index("sec"), lax.axis_index("day")
    sblocks, _, width = sec_ref.shape
    slots = hold_ref.shape[0]
    tail, portfolios = days_ref.shape
    pblocks = portfolios // PB
    rows = portfolios // n_sec
    own = slots // n_day
    bits = width // WORDS

    fetch_days = pltpu.make_async_copy(days_hbm, days_ref, load.at[0])
    fetch_sec = pltpu.make_async_copy(sec_hbm, sec_ref, load.at[1])
    fetch_hold = pltpu.make_async_copy(hold_hbm, hold_ref, load.at[2])
    fetch_days.start()
    fetch_sec.start()
    fetch_hold.start()

    barrier = pltpu.get_barrier_semaphore()
    for r in range(1, n_sec):
        pl.semaphore_signal(
            barrier, inc=1, device_id={"sec": lax.rem(sec + r, n_sec)}, device_id_type=MESH
        )
    for r in range(1, n_day):
        pl.semaphore_signal(
            barrier, inc=1, device_id={"day": lax.rem(day + r, n_day)}, device_id_type=MESH
        )

    fetch_days.wait()
    here = days_ref[...] - day * width
    inside = (here >= 0) & (here < width)
    word = jnp.where(inside, here & (WORDS - 1), -1)
    bit = jnp.left_shift(1, jnp.where(inside, here >> 4, 0))
    which = lax.broadcasted_iota(jnp.int32, (WORDS, portfolios), 0)
    packed = jnp.zeros((WORDS, portfolios), jnp.int32)
    for k in range(tail):
        packed = packed | jnp.where(which == word[k : k + 1, :], bit[k : k + 1, :], 0)
    for b in range(bits):
        piece = ((packed >> b) & 1).astype(F32).astype(jnp.bfloat16)
        for p in range(pblocks):
            mask_t[p, b * WORDS : (b + 1) * WORDS, :] = piece[:, p * PB : (p + 1) * PB]

    peak_out[...] = jnp.zeros(peak_out.shape, F32)

    fetch_sec.wait()
    pl.semaphore_wait(barrier, n_sec - 1 + n_day - 1)

    def tail_sum(slot):
        block = sec_ref[sblock_ref[slot]]
        return jnp.dot(block, mask_t[pblock_ref[slot]], preferred_element_type=F32)

    sends = []

    def send(src, dst, send_sem, recv_sem, where):
        copy = pltpu.make_async_remote_copy(
            src_ref=src,
            dst_ref=dst,
            send_sem=send_sem,
            recv_sem=recv_sem,
            device_id=where,
            device_id_type=MESH,
        )
        copy.start()
        sends.append(copy)
        return copy

    peak_copies, tail_copies = {}, {}
    for i in range(own):
        for r in range(1, n_day):
            to = lax.rem(day + r, n_day)
            at = (r - 1) * own + i
            sums = tail_sum(to * own + i)
            peak = jnp.maximum(jnp.max(jnp.abs(sums), axis=0, keepdims=True), 1e-30)
            peak_out[r - 1, i : i + 1, :] = peak
            tail_out[at] = jnp.round(sums * (REACH / peak)).astype(jnp.int32).astype(WIRE)
            tail_copies[r, i] = send(
                tail_out.at[at], tail_in.at[at], tail_send.at[at], tail_recv.at[at], {"day": to}
            )
    for r in range(1, n_day):
        to = lax.rem(day + r, n_day)
        peak_copies[r] = send(
            peak_out.at[r - 1], peak_in.at[r - 1], peak_send.at[r - 1], peak_recv.at[r - 1],
            {"day": to},
        )

    fetch_hold.wait()
    for t in range(slots):
        tile = hold_ref[t]
        home = jnp.where(t < count_ref[0], pblock_ref[t], -1)
        for p in range(pblocks):
            keep = (jnp.full((1, SB), home, jnp.int32) == p).astype(F32).astype(jnp.bfloat16)
            dense[p * PB : (p + 1) * PB, t * SB : (t + 1) * SB] = tile * keep
        held[t * SB : (t + 1) * SB, :] = sec_ref[sblock_ref[t]]
    part[...] = jnp.dot(dense[...], held[...], preferred_element_type=F32)

    share_copies = []
    for r in range(1, n_sec):
        to = lax.rem(sec + r, n_sec)
        share_copies.append(
            send(
                part.at[pl.ds(pl.multiple_of(to * rows, rows), rows), :],
                share_in.at[r - 1],
                share_send.at[r - 1],
                share_recv.at[r - 1],
                {"sec": to},
            )
        )

    for i in range(own):
        tail_own[i] = tail_sum(day * own + i)

    share = part[pl.ds(pl.multiple_of(sec * rows, rows), rows), :]
    for r in range(1, n_sec):
        share_copies[r - 1].wait_recv()
        share = share + share_in[r - 1]
    pnl_ref[...] = share.astype(jnp.bfloat16)
    high = share.astype(jnp.bfloat16)
    low = (share - high.astype(F32)).astype(jnp.bfloat16)
    lane = lax.broadcasted_iota(jnp.int32, (rows, PB), 1)
    line = lax.broadcasted_iota(jnp.int32, (rows, PB), 0)
    picked = []
    for p in range(pblocks):
        sums = jnp.dot(high, mask_t[p], preferred_element_type=F32)
        sums = sums + jnp.dot(low, mask_t[p], preferred_element_type=F32)
        mine = lane + p * PB == line + sec * rows
        picked.append(jnp.sum(jnp.where(mine, sums, 0.0), axis=0, keepdims=True))
    pick_out[...] = jnp.broadcast_to(jnp.concatenate(picked, axis=1), pick_out.shape)
    pick_copies = {}
    for r in range(1, n_day):
        to = lax.rem(day + r, n_day)
        pick_copies[r] = send(
            pick_out, pick_in.at[r - 1], pick_send.at[r - 1], pick_recv.at[r - 1], {"day": to}
        )

    back = {}
    for r in range(1, n_day):
        peak_copies[r].wait_recv()
        back[r] = peak_in[r - 1] * (1.0 / REACH)
    for i in range(own):
        total = tail_own[i]
        for r in range(1, n_day):
            tail_copies[r, i].wait_recv()
            coded = tail_in[(r - 1) * own + i].astype(jnp.int32).astype(F32)
            total = total + coded * back[r][i : i + 1, :]
        live = jnp.where(day * own + i < count_ref[0], 1.0, 0.0)
        tail_ref[i] = jnp.transpose(total) * (live / tail)

    lost = pick_out[...]
    for r in range(1, n_day):
        pick_copies[r].wait_recv()
        lost = lost + pick_in[r - 1]
    turned = pltpu.roll(lost, lax.rem(portfolios - sec * rows, portfolios), 1)
    short_ref[...] = turned[0:1, 0:rows] * (-1.0 / tail)
    for copy in sends:
        copy.wait_send()


def write_out(pnl_ref, short_ref, tail_ref, pnl_hbm, short_hbm, tail_hbm, store):
    copies = [
        pltpu.make_async_copy(tail_ref, tail_hbm, store.at[0]),
        pltpu.make_async_copy(pnl_ref, pnl_hbm, store.at[1]),
        pltpu.make_async_copy(short_ref, short_hbm, store.at[2]),
    ]
    for copy in copies:
        copy.start()
    for copy in copies:
        copy.wait()


def local(n_sec, n_day, sec_pnl, holdings, tile_pblock, tile_sblock, tile_count, tail_days):
    width = sec_pnl.shape[1]
    slots = holdings.shape[0]
    portfolios = tail_days.shape[0]
    rows, own = portfolios // n_sec, slots // n_day
    far = n_day - 1
    peak_rows = -(-own // 8) * 8
    smem, vmem = pl.BlockSpec(memory_space=pltpu.SMEM), pl.BlockSpec(memory_space=pltpu.VMEM)
    dma = pltpu.SemaphoreType.DMA
    anywhere = pl.BlockSpec(memory_space=pl.ANY)
    made = (
        jax.ShapeDtypeStruct((rows, width), jnp.bfloat16),
        jax.ShapeDtypeStruct((1, rows), F32),
        jax.ShapeDtypeStruct((own, PB, SB), F32),
    )
    inner = pl.pallas_call(
        functools.partial(kernel, n_sec, n_day),
        out_shape=made,
        in_specs=[smem] * 3 + [pl.BlockSpec(memory_space=pltpu.HBM)] * 3,
        out_specs=(vmem, vmem, vmem),
        scratch_shapes=[
            pltpu.VMEM((sec_pnl.shape[0] // SB, SB, width), sec_pnl.dtype),
            pltpu.VMEM(holdings.shape, holdings.dtype),
            pltpu.VMEM(tail_days.shape[::-1], tail_days.dtype),
            pltpu.VMEM((portfolios, slots * SB), jnp.bfloat16),
            pltpu.VMEM((slots * SB, width), jnp.bfloat16),
            pltpu.VMEM((portfolios, width), F32),
            pltpu.VMEM((n_sec - 1, rows, width), F32),
            pltpu.VMEM((portfolios // PB, width, PB), jnp.bfloat16),
            pltpu.VMEM((own, SB, PB), F32),
            pltpu.VMEM((far * own, SB, PB), WIRE),
            pltpu.VMEM((far * own, SB, PB), WIRE),
            pltpu.VMEM((far, peak_rows, PB), F32),
            pltpu.VMEM((far, peak_rows, PB), F32),
            pltpu.VMEM((8, portfolios), F32),
            pltpu.VMEM((far, 8, portfolios), F32),
            dma((3,)),
            dma((n_sec - 1,)),
            dma((n_sec - 1,)),
            dma((far * own,)),
            dma((far * own,)),
            dma((far,)),
            dma((far,)),
            dma((far,)),
            dma((far,)),
        ],
        compiler_params=pltpu.CompilerParams(
            collective_id=0, has_side_effects=True, vmem_limit_bytes=62 * 1024 * 1024
        ),
    )(tile_pblock, tile_sblock, tile_count, sec_pnl.reshape(-1, SB, width), holdings, tail_days.T)
    pnl, short, tail = pl.pallas_call(
        write_out,
        out_shape=made,
        in_specs=[anywhere] * 3,
        out_specs=(anywhere,) * 3,
        scratch_shapes=[dma((3,))],
        compiler_params=pltpu.CompilerParams(vmem_limit_bytes=62 * 1024 * 1024),
    )(*inner)
    return pnl, short.reshape(rows), tail


def solution(mesh):
    placed = (P("sec", "day"), P("sec", None, None), P("sec"), P("sec"), P("sec"), P())
    return jax.shard_map(
        functools.partial(local, mesh.shape["sec"], mesh.shape["day"]),
        mesh=mesh,
        in_specs=placed,
        out_specs=(P("sec", "day"), P("sec"), P(("sec", "day"), None, None)),
        check_vma=False,
    )
```

```python
import functools

import jax
import jax.numpy as jnp
from jax import lax
from jax.experimental import pallas as pl
from jax.experimental.pallas import tpu as pltpu
from jax.sharding import PartitionSpec as P

SB = 128
PB = 128
WORDS = 16
WIRE = jnp.int16
REACH = 32767.0
F32 = jnp.float32
MESH = pl.DeviceIdType.MESH


def kernel(
    n_sec,
    n_day,
    pblock_ref,
    sblock_ref,
    count_ref,
    sec_hbm,
    hold_hbm,
    days_hbm,
    pnl_ref,
    short_ref,
    tail_ref,
    sec_ref,
    hold_ref,
    days_ref,
    dense,
    held,
    part,
    share_in,
    mask_t,
    tail_own,
    tail_out,
    tail_in,
    peak_out,
    peak_in,
    pick_out,
    pick_in,
    load,
    share_send,
    share_recv,
    tail_send,
    tail_recv,
    peak_send,
    peak_recv,
    pick_send,
    pick_recv,
):
    sec, day = lax.axis_index("sec"), lax.axis_index("day")
    sblocks, _, width = sec_ref.shape
    slots = hold_ref.shape[0]
    tail, portfolios = days_ref.shape
    pblocks = portfolios // PB
    rows = portfolios // n_sec
    own = slots // n_day
    bits = width // WORDS

    fetch_days = pltpu.make_async_copy(days_hbm, days_ref, load.at[0])
    fetch_sec = pltpu.make_async_copy(sec_hbm, sec_ref, load.at[1])
    fetch_hold = pltpu.make_async_copy(hold_hbm, hold_ref, load.at[2])
    fetch_days.start()
    fetch_sec.start()
    fetch_hold.start()

    barrier = pltpu.get_barrier_semaphore()
    for r in range(1, n_sec):
        pl.semaphore_signal(
            barrier, inc=1, device_id={"sec": lax.rem(sec + r, n_sec)}, device_id_type=MESH
        )
    for r in range(1, n_day):
        pl.semaphore_signal(
            barrier, inc=1, device_id={"day": lax.rem(day + r, n_day)}, device_id_type=MESH
        )

    fetch_days.wait()
    here = days_ref[...] - day * width
    inside = (here >= 0) & (here < width)
    word = jnp.where(inside, here & (WORDS - 1), -1)
    bit = jnp.left_shift(1, jnp.where(inside, here >> 4, 0))
    which = lax.broadcasted_iota(jnp.int32, (WORDS, portfolios), 0)
    packed = jnp.zeros((WORDS, portfolios), jnp.int32)
    for k in range(tail):
        packed = packed | jnp.where(which == word[k : k + 1, :], bit[k : k + 1, :], 0)
    for b in range(bits):
        piece = ((packed >> b) & 1).astype(F32).astype(jnp.bfloat16)
        for p in range(pblocks):
            mask_t[p, b * WORDS : (b + 1) * WORDS, :] = piece[:, p * PB : (p + 1) * PB]

    peak_out[...] = jnp.zeros(peak_out.shape, F32)

    fetch_sec.wait()
    pl.semaphore_wait(barrier, n_sec - 1 + n_day - 1)

    def tail_sum(slot):
        block = sec_ref[sblock_ref[slot]]
        return jnp.dot(block, mask_t[pblock_ref[slot]], preferred_element_type=F32)

    sends = []

    def send(src, dst, send_sem, recv_sem, where):
        copy = pltpu.make_async_remote_copy(
            src_ref=src,
            dst_ref=dst,
            send_sem=send_sem,
            recv_sem=recv_sem,
            device_id=where,
            device_id_type=MESH,
        )
        copy.start()
        sends.append(copy)
        return copy

    peak_copies, tail_copies = {}, {}
    for i in range(own):
        for r in range(1, n_day):
            to = lax.rem(day + r, n_day)
            at = (r - 1) * own + i
            sums = tail_sum(to * own + i)
            peak = jnp.maximum(jnp.max(jnp.abs(sums), axis=0, keepdims=True), 1e-30)
            peak_out[r - 1, i : i + 1, :] = peak
            tail_out[at] = jnp.round(sums * (REACH / peak)).astype(jnp.int32).astype(WIRE)
            tail_copies[r, i] = send(
                tail_out.at[at], tail_in.at[at], tail_send.at[at], tail_recv.at[at], {"day": to}
            )
    for r in range(1, n_day):
        to = lax.rem(day + r, n_day)
        peak_copies[r] = send(
            peak_out.at[r - 1], peak_in.at[r - 1], peak_send.at[r - 1], peak_recv.at[r - 1],
            {"day": to},
        )

    fetch_hold.wait()
    for t in range(slots):
        tile = hold_ref[t]
        home = jnp.where(t < count_ref[0], pblock_ref[t], -1)
        for p in range(pblocks):
            keep = (jnp.full((1, SB), home, jnp.int32) == p).astype(F32).astype(jnp.bfloat16)
            dense[p * PB : (p + 1) * PB, t * SB : (t + 1) * SB] = tile * keep
        held[t * SB : (t + 1) * SB, :] = sec_ref[sblock_ref[t]]
    part[...] = jnp.dot(dense[...], held[...], preferred_element_type=F32)

    share_copies = []
    for r in range(1, n_sec):
        to = lax.rem(sec + r, n_sec)
        share_copies.append(
            send(
                part.at[pl.ds(pl.multiple_of(to * rows, rows), rows), :],
                share_in.at[r - 1],
                share_send.at[r - 1],
                share_recv.at[r - 1],
                {"sec": to},
            )
        )

    for i in range(own):
        tail_own[i] = tail_sum(day * own + i)

    share = part[pl.ds(pl.multiple_of(sec * rows, rows), rows), :]
    for r in range(1, n_sec):
        share_copies[r - 1].wait_recv()
        share = share + share_in[r - 1]
    pnl_ref[...] = share.astype(jnp.bfloat16)
    high = share.astype(jnp.bfloat16)
    low = (share - high.astype(F32)).astype(jnp.bfloat16)
    lane = lax.broadcasted_iota(jnp.int32, (rows, PB), 1)
    line = lax.broadcasted_iota(jnp.int32, (rows, PB), 0)
    picked = []
    for p in range(pblocks):
        sums = jnp.dot(high, mask_t[p], preferred_element_type=F32)
        sums = sums + jnp.dot(low, mask_t[p], preferred_element_type=F32)
        mine = lane + p * PB == line + sec * rows
        picked.append(jnp.sum(jnp.where(mine, sums, 0.0), axis=0, keepdims=True))
    pick_out[...] = jnp.broadcast_to(jnp.concatenate(picked, axis=1), pick_out.shape)
    pick_copies = {}
    for r in range(1, n_day):
        to = lax.rem(day + r, n_day)
        pick_copies[r] = send(
            pick_out, pick_in.at[r - 1], pick_send.at[r - 1], pick_recv.at[r - 1], {"day": to}
        )

    back = {}
    for r in range(1, n_day):
        peak_copies[r].wait_recv()
        back[r] = peak_in[r - 1] * (1.0 / REACH)
    for i in range(own):
        total = tail_own[i]
        for r in range(1, n_day):
            tail_copies[r, i].wait_recv()
            coded = tail_in[(r - 1) * own + i].astype(jnp.int32).astype(F32)
            total = total + coded * back[r][i : i + 1, :]
        live = jnp.where(day * own + i < count_ref[0], 1.0, 0.0)
        tail_ref[i] = jnp.transpose(total) * (live / tail)

    lost = pick_out[...]
    for r in range(1, n_day):
        pick_copies[r].wait_recv()
        lost = lost + pick_in[r - 1]
    turned = pltpu.roll(lost, lax.rem(portfolios - sec * rows, portfolios), 1)
    short_ref[...] = turned[0:1, 0:rows] * (-1.0 / tail)
    for copy in sends:
        copy.wait_send()


def write_out(pnl_ref, short_ref, tail_ref, pnl_hbm, short_hbm, tail_hbm, store):
    copies = [
        pltpu.make_async_copy(tail_ref, tail_hbm, store.at[0]),
        pltpu.make_async_copy(pnl_ref, pnl_hbm, store.at[1]),
        pltpu.make_async_copy(short_ref, short_hbm, store.at[2]),
    ]
    for copy in copies:
        copy.start()
    for copy in copies:
        copy.wait()


def local(n_sec, n_day, sec_pnl, holdings, tile_pblock, tile_sblock, tile_count, tail_days):
    width = sec_pnl.shape[1]
    slots = holdings.shape[0]
    portfolios = tail_days.shape[0]
    rows, own = portfolios // n_sec, slots // n_day
    far = n_day - 1
    peak_rows = -(-own // 8) * 8
    smem, vmem = pl.BlockSpec(memory_space=pltpu.SMEM), pl.BlockSpec(memory_space=pltpu.VMEM)
    dma = pltpu.SemaphoreType.DMA
    anywhere = pl.BlockSpec(memory_space=pl.ANY)
    made = (
        jax.ShapeDtypeStruct((rows, width), jnp.bfloat16),
        jax.ShapeDtypeStruct((1, rows), F32),
        jax.ShapeDtypeStruct((own, PB, SB), F32),
    )
    inner = pl.pallas_call(
        functools.partial(kernel, n_sec, n_day),
        out_shape=made,
        in_specs=[smem] * 3 + [pl.BlockSpec(memory_space=pltpu.HBM)] * 3,
        out_specs=(vmem, vmem, vmem),
        scratch_shapes=[
            pltpu.VMEM((sec_pnl.shape[0] // SB, SB, width), sec_pnl.dtype),
            pltpu.VMEM(holdings.shape, holdings.dtype),
            pltpu.VMEM(tail_days.shape[::-1], tail_days.dtype),
            pltpu.VMEM((portfolios, slots * SB), jnp.bfloat16),
            pltpu.VMEM((slots * SB, width), jnp.bfloat16),
            pltpu.VMEM((portfolios, width), F32),
            pltpu.VMEM((n_sec - 1, rows, width), F32),
            pltpu.VMEM((portfolios // PB, width, PB), jnp.bfloat16),
            pltpu.VMEM((own, SB, PB), F32),
            pltpu.VMEM((far * own, SB, PB), WIRE),
            pltpu.VMEM((far * own, SB, PB), WIRE),
            pltpu.VMEM((far, peak_rows, PB), F32),
            pltpu.VMEM((far, peak_rows, PB), F32),
            pltpu.VMEM((8, portfolios), F32),
            pltpu.VMEM((far, 8, portfolios), F32),
            dma((3,)),
            dma((n_sec - 1,)),
            dma((n_sec - 1,)),
            dma((far * own,)),
            dma((far * own,)),
            dma((far,)),
            dma((far,)),
            dma((far,)),
            dma((far,)),
        ],
        compiler_params=pltpu.CompilerParams(
            collective_id=0, has_side_effects=True, vmem_limit_bytes=57 * 1024 * 1024
        ),
    )(tile_pblock, tile_sblock, tile_count, sec_pnl.reshape(-1, SB, width), holdings, tail_days.T)
    pnl, short, tail = pl.pallas_call(
        write_out,
        out_shape=made,
        in_specs=[anywhere] * 3,
        out_specs=(anywhere,) * 3,
        scratch_shapes=[dma((3,))],
        compiler_params=pltpu.CompilerParams(vmem_limit_bytes=4 * 1024 * 1024),
    )(*inner)
    return pnl, short.reshape(rows), tail


def solution(mesh):
    placed = (P("sec", "day"), P("sec", None, None), P("sec"), P("sec"), P("sec"), P())
    return jax.shard_map(
        functools.partial(local, mesh.shape["sec"], mesh.shape["day"]),
        mesh=mesh,
        in_specs=placed,
        out_specs=(P("sec", "day"), P("sec"), P(("sec", "day"), None, None)),
        check_vma=False,
    )
```

```python
import functools

import jax
import jax.numpy as jnp
from jax import lax
from jax.experimental import pallas as pl
from jax.experimental.pallas import tpu as pltpu
from jax.sharding import PartitionSpec as P

SB = 128
PB = 128
WORDS = 16
WIRE = jnp.int16
REACH = 32767.0
F32 = jnp.float32
MESH = pl.DeviceIdType.MESH


def kernel(
    n_sec,
    n_day,
    pblock_ref,
    sblock_ref,
    count_ref,
    sec_hbm,
    hold_hbm,
    days_hbm,
    pnl_ref,
    short_ref,
    tail_ref,
    sec_ref,
    hold_ref,
    days_ref,
    dense,
    held,
    part,
    share_in,
    mask_t,
    tail_own,
    tail_out,
    tail_in,
    peak_out,
    peak_in,
    pick_out,
    pick_in,
    load,
    share_send,
    share_recv,
    tail_send,
    tail_recv,
    peak_send,
    peak_recv,
    pick_send,
    pick_recv,
):
    sec, day = lax.axis_index("sec"), lax.axis_index("day")
    sblocks, _, width = sec_ref.shape
    slots = hold_ref.shape[0]
    tail, portfolios = days_ref.shape
    pblocks = portfolios // PB
    rows = portfolios // n_sec
    own = slots // n_day
    bits = width // WORDS

    fetch_days = pltpu.make_async_copy(days_hbm, days_ref, load.at[0])
    fetch_sec = pltpu.make_async_copy(sec_hbm, sec_ref, load.at[1])
    fetch_hold = pltpu.make_async_copy(hold_hbm, hold_ref, load.at[2])
    fetch_days.start()
    fetch_sec.start()
    fetch_hold.start()

    barrier = pltpu.get_barrier_semaphore()
    for r in range(1, n_sec):
        pl.semaphore_signal(
            barrier, inc=1, device_id={"sec": lax.rem(sec + r, n_sec)}, device_id_type=MESH
        )
    for r in range(1, n_day):
        pl.semaphore_signal(
            barrier, inc=1, device_id={"day": lax.rem(day + r, n_day)}, device_id_type=MESH
        )

    fetch_days.wait()
    here = days_ref[...] - day * width
    inside = (here >= 0) & (here < width)
    word = jnp.where(inside, here & (WORDS - 1), -1)
    bit = jnp.left_shift(1, jnp.where(inside, here >> 4, 0))
    which = lax.broadcasted_iota(jnp.int32, (WORDS, portfolios), 0)
    packed = jnp.zeros((WORDS, portfolios), jnp.int32)
    for k in range(tail):
        packed = packed | jnp.where(which == word[k : k + 1, :], bit[k : k + 1, :], 0)
    for b in range(bits):
        piece = ((packed >> b) & 1).astype(F32).astype(jnp.bfloat16)
        for p in range(pblocks):
            mask_t[p, b * WORDS : (b + 1) * WORDS, :] = piece[:, p * PB : (p + 1) * PB]

    peak_out[...] = jnp.zeros(peak_out.shape, F32)

    fetch_sec.wait()
    pl.semaphore_wait(barrier, n_sec - 1 + n_day - 1)

    def tail_sum(slot):
        block = sec_ref[sblock_ref[slot]]
        return jnp.dot(block, mask_t[pblock_ref[slot]], preferred_element_type=F32)

    sends = []

    def send(src, dst, send_sem, recv_sem, where):
        copy = pltpu.make_async_remote_copy(
            src_ref=src,
            dst_ref=dst,
            send_sem=send_sem,
            recv_sem=recv_sem,
            device_id=where,
            device_id_type=MESH,
        )
        copy.start()
        sends.append(copy)
        return copy

    peak_copies, tail_copies = {}, {}
    for i in range(own):
        for r in range(1, n_day):
            to = lax.rem(day + r, n_day)
            at = (r - 1) * own + i
            sums = tail_sum(to * own + i)
            peak = jnp.maximum(jnp.max(jnp.abs(sums), axis=0, keepdims=True), 1e-30)
            peak_out[r - 1, i : i + 1, :] = peak
            tail_out[at] = jnp.round(sums * (REACH / peak)).astype(jnp.int32).astype(WIRE)
            tail_copies[r, i] = send(
                tail_out.at[at], tail_in.at[at], tail_send.at[at], tail_recv.at[at], {"day": to}
            )
    for r in range(1, n_day):
        to = lax.rem(day + r, n_day)
        peak_copies[r] = send(
            peak_out.at[r - 1], peak_in.at[r - 1], peak_send.at[r - 1], peak_recv.at[r - 1],
            {"day": to},
        )

    fetch_hold.wait()
    for t in range(slots):
        tile = hold_ref[t]
        home = jnp.where(t < count_ref[0], pblock_ref[t], -1)
        for p in range(pblocks):
            keep = (jnp.full((1, SB), home, jnp.int32) == p).astype(F32).astype(jnp.bfloat16)
            dense[p * PB : (p + 1) * PB, t * SB : (t + 1) * SB] = tile * keep
        held[t * SB : (t + 1) * SB, :] = sec_ref[sblock_ref[t]]
    part[...] = jnp.dot(dense[...], held[...], preferred_element_type=F32)

    share_copies = []
    for r in range(1, n_sec):
        to = lax.rem(sec + r, n_sec)
        share_copies.append(
            send(
                part.at[pl.ds(pl.multiple_of(to * rows, rows), rows), :],
                share_in.at[r - 1],
                share_send.at[r - 1],
                share_recv.at[r - 1],
                {"sec": to},
            )
        )

    for i in range(own):
        tail_own[i] = tail_sum(day * own + i)

    share = part[pl.ds(pl.multiple_of(sec * rows, rows), rows), :]
    for r in range(1, n_sec):
        share_copies[r - 1].wait_recv()
        share = share + share_in[r - 1]
    pnl_ref[...] = share.astype(jnp.bfloat16)
    high = share.astype(jnp.bfloat16)
    low = (share - high.astype(F32)).astype(jnp.bfloat16)
    lane = lax.broadcasted_iota(jnp.int32, (rows, PB), 1)
    line = lax.broadcasted_iota(jnp.int32, (rows, PB), 0)
    picked = []
    for p in range(pblocks):
        sums = jnp.dot(high, mask_t[p], preferred_element_type=F32)
        sums = sums + jnp.dot(low, mask_t[p], preferred_element_type=F32)
        mine = lane + p * PB == line + sec * rows
        picked.append(jnp.sum(jnp.where(mine, sums, 0.0), axis=0, keepdims=True))
    pick_out[...] = jnp.broadcast_to(jnp.concatenate(picked, axis=1), pick_out.shape)
    pick_copies = {}
    for r in range(1, n_day):
        to = lax.rem(day + r, n_day)
        pick_copies[r] = send(
            pick_out, pick_in.at[r - 1], pick_send.at[r - 1], pick_recv.at[r - 1], {"day": to}
        )

    back = {}
    for r in range(1, n_day):
        peak_copies[r].wait_recv()
        back[r] = peak_in[r - 1] * (1.0 / REACH)
    for i in range(own):
        total = tail_own[i]
        for r in range(1, n_day):
            tail_copies[r, i].wait_recv()
            coded = tail_in[(r - 1) * own + i].astype(jnp.int32).astype(F32)
            total = total + coded * back[r][i : i + 1, :]
        live = jnp.where(day * own + i < count_ref[0], 1.0, 0.0)
        tail_ref[i] = jnp.transpose(total) * (live / tail)

    lost = pick_out[...]
    for r in range(1, n_day):
        pick_copies[r].wait_recv()
        lost = lost + pick_in[r - 1]
    turned = pltpu.roll(lost, lax.rem(portfolios - sec * rows, portfolios), 1)
    short_ref[...] = turned[0:1, 0:rows] * (-1.0 / tail)
    for copy in sends:
        copy.wait_send()


def write_out(pnl_ref, short_ref, tail_ref, pnl_hbm, short_hbm, tail_hbm, store):
    copies = [
        pltpu.make_async_copy(tail_ref, tail_hbm, store.at[0]),
        pltpu.make_async_copy(pnl_ref, pnl_hbm, store.at[1]),
        pltpu.make_async_copy(short_ref, short_hbm, store.at[2]),
    ]
    for copy in copies:
        copy.start()
    for copy in copies:
        copy.wait()


def local(n_sec, n_day, sec_pnl, holdings, tile_pblock, tile_sblock, tile_count, tail_days):
    width = sec_pnl.shape[1]
    slots = holdings.shape[0]
    portfolios = tail_days.shape[0]
    rows, own = portfolios // n_sec, slots // n_day
    far = n_day - 1
    peak_rows = -(-own // 8) * 8
    smem, vmem = pl.BlockSpec(memory_space=pltpu.SMEM), pl.BlockSpec(memory_space=pltpu.VMEM)
    dma = pltpu.SemaphoreType.DMA
    anywhere = pl.BlockSpec(memory_space=pl.ANY)
    made = (
        jax.ShapeDtypeStruct((rows, width), jnp.bfloat16),
        jax.ShapeDtypeStruct((1, rows), F32),
        jax.ShapeDtypeStruct((own, PB, SB), F32),
    )
    inner = pl.pallas_call(
        functools.partial(kernel, n_sec, n_day),
        out_shape=tuple(pltpu.VMEM(m.shape, m.dtype) for m in made),
        in_specs=[smem] * 3 + [pl.BlockSpec(memory_space=pltpu.HBM)] * 3,
        out_specs=(vmem, vmem, vmem),
        scratch_shapes=[
            pltpu.VMEM((sec_pnl.shape[0] // SB, SB, width), sec_pnl.dtype),
            pltpu.VMEM(holdings.shape, holdings.dtype),
            pltpu.VMEM(tail_days.shape[::-1], tail_days.dtype),
            pltpu.VMEM((portfolios, slots * SB), jnp.bfloat16),
            pltpu.VMEM((slots * SB, width), jnp.bfloat16),
            pltpu.VMEM((portfolios, width), F32),
            pltpu.VMEM((n_sec - 1, rows, width), F32),
            pltpu.VMEM((portfolios // PB, width, PB), jnp.bfloat16),
            pltpu.VMEM((own, SB, PB), F32),
            pltpu.VMEM((far * own, SB, PB), WIRE),
            pltpu.VMEM((far * own, SB, PB), WIRE),
            pltpu.VMEM((far, peak_rows, PB), F32),
            pltpu.VMEM((far, peak_rows, PB), F32),
            pltpu.VMEM((8, portfolios), F32),
            pltpu.VMEM((far, 8, portfolios), F32),
            dma((3,)),
            dma((n_sec - 1,)),
            dma((n_sec - 1,)),
            dma((far * own,)),
            dma((far * own,)),
            dma((far,)),
            dma((far,)),
            dma((far,)),
            dma((far,)),
        ],
        compiler_params=pltpu.CompilerParams(
            collective_id=0, has_side_effects=True, vmem_limit_bytes=57 * 1024 * 1024
        ),
    )(tile_pblock, tile_sblock, tile_count, sec_pnl.reshape(-1, SB, width), holdings, tail_days.T)
    pnl, short, tail = pl.pallas_call(
        write_out,
        out_shape=made,
        in_specs=[anywhere] * 3,
        out_specs=(anywhere,) * 3,
        scratch_shapes=[dma((3,))],
        compiler_params=pltpu.CompilerParams(vmem_limit_bytes=4 * 1024 * 1024),
    )(*inner)
    return pnl, short.reshape(rows), tail


def solution(mesh):
    placed = (P("sec", "day"), P("sec", None, None), P("sec"), P("sec"), P("sec"), P())
    return jax.shard_map(
        functools.partial(local, mesh.shape["sec"], mesh.shape["day"]),
        mesh=mesh,
        in_specs=placed,
        out_specs=(P("sec", "day"), P("sec"), P(("sec", "day"), None, None)),
        check_vma=False,
    )
```

```python
import functools

import jax
import jax.numpy as jnp
from jax import lax
from jax.experimental import pallas as pl
from jax.experimental.pallas import tpu as pltpu
from jax.sharding import PartitionSpec as P

SB = 128
PB = 128
WORDS = 16
WIRE = jnp.int16
REACH = 32767.0
F32 = jnp.float32
MESH = pl.DeviceIdType.MESH


def kernel(
    n_sec,
    n_day,
    pblock_ref,
    sblock_ref,
    count_ref,
    sec_hbm,
    hold_hbm,
    days_hbm,
    pnl_ref,
    short_ref,
    tail_ref,
    sec_ref,
    hold_ref,
    days_ref,
    dense,
    held,
    part,
    share_in,
    mask_t,
    tail_own,
    tail_out,
    tail_in,
    peak_out,
    peak_in,
    pick_out,
    pick_in,
    load,
    share_send,
    share_recv,
    tail_send,
    tail_recv,
    peak_send,
    peak_recv,
    pick_send,
    pick_recv,
):
    sec, day = lax.axis_index("sec"), lax.axis_index("day")
    sblocks, _, width = sec_ref.shape
    slots = hold_ref.shape[0]
    tail, portfolios = days_ref.shape
    pblocks = portfolios // PB
    rows = portfolios // n_sec
    own = slots // n_day
    bits = width // WORDS

    fetch_days = pltpu.make_async_copy(days_hbm, days_ref, load.at[0])
    fetch_sec = pltpu.make_async_copy(sec_hbm, sec_ref, load.at[1])
    fetch_hold = pltpu.make_async_copy(hold_hbm, hold_ref, load.at[2])
    fetch_days.start()
    fetch_sec.start()
    fetch_hold.start()

    barrier = pltpu.get_barrier_semaphore()
    for r in range(1, n_sec):
        pl.semaphore_signal(
            barrier, inc=1, device_id={"sec": lax.rem(sec + r, n_sec)}, device_id_type=MESH
        )
    for r in range(1, n_day):
        pl.semaphore_signal(
            barrier, inc=1, device_id={"day": lax.rem(day + r, n_day)}, device_id_type=MESH
        )

    fetch_days.wait()
    here = days_ref[...] - day * width
    inside = (here >= 0) & (here < width)
    word = jnp.where(inside, here & (WORDS - 1), -1)
    bit = jnp.left_shift(1, jnp.where(inside, here >> 4, 0))
    which = lax.broadcasted_iota(jnp.int32, (WORDS, portfolios), 0)
    packed = jnp.zeros((WORDS, portfolios), jnp.int32)
    for k in range(tail):
        packed = packed | jnp.where(which == word[k : k + 1, :], bit[k : k + 1, :], 0)
    for b in range(bits):
        piece = ((packed >> b) & 1).astype(F32).astype(jnp.bfloat16)
        for p in range(pblocks):
            mask_t[p, b * WORDS : (b + 1) * WORDS, :] = piece[:, p * PB : (p + 1) * PB]

    peak_out[...] = jnp.zeros(peak_out.shape, F32)

    fetch_sec.wait()
    pl.semaphore_wait(barrier, n_sec - 1 + n_day - 1)

    def tail_sum(slot):
        block = sec_ref[sblock_ref[slot]]
        return jnp.dot(block, mask_t[pblock_ref[slot]], preferred_element_type=F32)

    sends = []

    def send(src, dst, send_sem, recv_sem, where):
        copy = pltpu.make_async_remote_copy(
            src_ref=src,
            dst_ref=dst,
            send_sem=send_sem,
            recv_sem=recv_sem,
            device_id=where,
            device_id_type=MESH,
        )
        copy.start()
        sends.append(copy)
        return copy

    peak_copies, tail_copies = {}, {}
    half = (own + 1) // 2
    for i in range(half):
        for r in range(1, n_day):
            to = lax.rem(day + r, n_day)
            at = (r - 1) * own + i
            sums = tail_sum(to * own + i)
            peak = jnp.maximum(jnp.max(jnp.abs(sums), axis=0, keepdims=True), 1e-30)
            peak_out[r - 1, i : i + 1, :] = peak
            tail_out[at] = jnp.round(sums * (REACH / peak)).astype(jnp.int32).astype(WIRE)
            tail_copies[r, i] = send(
                tail_out.at[at], tail_in.at[at], tail_send.at[at], tail_recv.at[at], {"day": to}
            )

    fetch_hold.wait()
    for t in range(slots):
        tile = hold_ref[t]
        home = jnp.where(t < count_ref[0], pblock_ref[t], -1)
        for p in range(pblocks):
            keep = (jnp.full((1, SB), home, jnp.int32) == p).astype(F32).astype(jnp.bfloat16)
            dense[p * PB : (p + 1) * PB, t * SB : (t + 1) * SB] = tile * keep
        held[t * SB : (t + 1) * SB, :] = sec_ref[sblock_ref[t]]
    part[...] = jnp.dot(dense[...], held[...], preferred_element_type=F32)

    share_copies = []
    for r in range(1, n_sec):
        to = lax.rem(sec + r, n_sec)
        share_copies.append(
            send(
                part.at[pl.ds(pl.multiple_of(to * rows, rows), rows), :],
                share_in.at[r - 1],
                share_send.at[r - 1],
                share_recv.at[r - 1],
                {"sec": to},
            )
        )

    for i in range(half, own):
        for r in range(1, n_day):
            to = lax.rem(day + r, n_day)
            at = (r - 1) * own + i
            sums = tail_sum(to * own + i)
            peak = jnp.maximum(jnp.max(jnp.abs(sums), axis=0, keepdims=True), 1e-30)
            peak_out[r - 1, i : i + 1, :] = peak
            tail_out[at] = jnp.round(sums * (REACH / peak)).astype(jnp.int32).astype(WIRE)
            tail_copies[r, i] = send(
                tail_out.at[at], tail_in.at[at], tail_send.at[at], tail_recv.at[at], {"day": to}
            )
    for r in range(1, n_day):
        to = lax.rem(day + r, n_day)
        peak_copies[r] = send(
            peak_out.at[r - 1], peak_in.at[r - 1], peak_send.at[r - 1], peak_recv.at[r - 1],
            {"day": to},
        )

    for i in range(own):
        tail_own[i] = tail_sum(day * own + i)

    share = part[pl.ds(pl.multiple_of(sec * rows, rows), rows), :]
    for r in range(1, n_sec):
        share_copies[r - 1].wait_recv()
        share = share + share_in[r - 1]
    pnl_ref[...] = share.astype(jnp.bfloat16)
    high = share.astype(jnp.bfloat16)
    low = (share - high.astype(F32)).astype(jnp.bfloat16)
    lane = lax.broadcasted_iota(jnp.int32, (rows, PB), 1)
    line = lax.broadcasted_iota(jnp.int32, (rows, PB), 0)
    picked = []
    for p in range(pblocks):
        sums = jnp.dot(high, mask_t[p], preferred_element_type=F32)
        sums = sums + jnp.dot(low, mask_t[p], preferred_element_type=F32)
        mine = lane + p * PB == line + sec * rows
        picked.append(jnp.sum(jnp.where(mine, sums, 0.0), axis=0, keepdims=True))
    pick_out[...] = jnp.broadcast_to(jnp.concatenate(picked, axis=1), pick_out.shape)
    pick_copies = {}
    for r in range(1, n_day):
        to = lax.rem(day + r, n_day)
        pick_copies[r] = send(
            pick_out, pick_in.at[r - 1], pick_send.at[r - 1], pick_recv.at[r - 1], {"day": to}
        )

    back = {}
    for r in range(1, n_day):
        peak_copies[r].wait_recv()
        back[r] = peak_in[r - 1] * (1.0 / REACH)
    for i in range(own):
        total = tail_own[i]
        for r in range(1, n_day):
            tail_copies[r, i].wait_recv()
            coded = tail_in[(r - 1) * own + i].astype(jnp.int32).astype(F32)
            total = total + coded * back[r][i : i + 1, :]
        live = jnp.where(day * own + i < count_ref[0], 1.0, 0.0)
        tail_ref[i] = jnp.transpose(total) * (live / tail)

    lost = pick_out[...]
    for r in range(1, n_day):
        pick_copies[r].wait_recv()
        lost = lost + pick_in[r - 1]
    turned = pltpu.roll(lost, lax.rem(portfolios - sec * rows, portfolios), 1)
    short_ref[...] = turned[0:1, 0:rows] * (-1.0 / tail)
    for copy in sends:
        copy.wait_send()


def write_out(pnl_ref, short_ref, tail_ref, pnl_hbm, short_hbm, tail_hbm, store):
    copies = [
        pltpu.make_async_copy(tail_ref, tail_hbm, store.at[0]),
        pltpu.make_async_copy(pnl_ref, pnl_hbm, store.at[1]),
        pltpu.make_async_copy(short_ref, short_hbm, store.at[2]),
    ]
    for copy in copies:
        copy.start()
    for copy in copies:
        copy.wait()


def local(n_sec, n_day, sec_pnl, holdings, tile_pblock, tile_sblock, tile_count, tail_days):
    width = sec_pnl.shape[1]
    slots = holdings.shape[0]
    portfolios = tail_days.shape[0]
    rows, own = portfolios // n_sec, slots // n_day
    far = n_day - 1
    peak_rows = -(-own // 8) * 8
    smem, vmem = pl.BlockSpec(memory_space=pltpu.SMEM), pl.BlockSpec(memory_space=pltpu.VMEM)
    dma = pltpu.SemaphoreType.DMA
    anywhere = pl.BlockSpec(memory_space=pl.ANY)
    made = (
        jax.ShapeDtypeStruct((rows, width), jnp.bfloat16),
        jax.ShapeDtypeStruct((1, rows), F32),
        jax.ShapeDtypeStruct((own, PB, SB), F32),
    )
    inner = pl.pallas_call(
        functools.partial(kernel, n_sec, n_day),
        out_shape=tuple(pltpu.VMEM(m.shape, m.dtype) for m in made),
        in_specs=[smem] * 3 + [pl.BlockSpec(memory_space=pltpu.HBM)] * 3,
        out_specs=(vmem, vmem, vmem),
        scratch_shapes=[
            pltpu.VMEM((sec_pnl.shape[0] // SB, SB, width), sec_pnl.dtype),
            pltpu.VMEM(holdings.shape, holdings.dtype),
            pltpu.VMEM(tail_days.shape[::-1], tail_days.dtype),
            pltpu.VMEM((portfolios, slots * SB), jnp.bfloat16),
            pltpu.VMEM((slots * SB, width), jnp.bfloat16),
            pltpu.VMEM((portfolios, width), F32),
            pltpu.VMEM((n_sec - 1, rows, width), F32),
            pltpu.VMEM((portfolios // PB, width, PB), jnp.bfloat16),
            pltpu.VMEM((own, SB, PB), F32),
            pltpu.VMEM((far * own, SB, PB), WIRE),
            pltpu.VMEM((far * own, SB, PB), WIRE),
            pltpu.VMEM((far, peak_rows, PB), F32),
            pltpu.VMEM((far, peak_rows, PB), F32),
            pltpu.VMEM((8, portfolios), F32),
            pltpu.VMEM((far, 8, portfolios), F32),
            dma((3,)),
            dma((n_sec - 1,)),
            dma((n_sec - 1,)),
            dma((far * own,)),
            dma((far * own,)),
            dma((far,)),
            dma((far,)),
            dma((far,)),
            dma((far,)),
        ],
        compiler_params=pltpu.CompilerParams(
            collective_id=0, has_side_effects=True, vmem_limit_bytes=57 * 1024 * 1024
        ),
    )(tile_pblock, tile_sblock, tile_count, sec_pnl.reshape(-1, SB, width), holdings, tail_days.T)
    pnl, short, tail = pl.pallas_call(
        write_out,
        out_shape=made,
        in_specs=[anywhere] * 3,
        out_specs=(anywhere,) * 3,
        scratch_shapes=[dma((3,))],
        compiler_params=pltpu.CompilerParams(vmem_limit_bytes=4 * 1024 * 1024),
    )(*inner)
    return pnl, short.reshape(rows), tail


def solution(mesh):
    placed = (P("sec", "day"), P("sec", None, None), P("sec"), P("sec"), P("sec"), P())
    return jax.shard_map(
        functools.partial(local, mesh.shape["sec"], mesh.shape["day"]),
        mesh=mesh,
        in_specs=placed,
        out_specs=(P("sec", "day"), P("sec"), P(("sec", "day"), None, None)),
        check_vma=False,
    )
```
